32 devices in a mesh: user: 2 (over x), item: 4 (over z), feat: 4 (over y, core).
Axes of the slice: x: 2, y: 2, z: 4, core: 2. Of those that a mesh axis runs over, the one named last changes fastest.
Arguments:
- tensor_tiles: bfloat16 [64, 256, 16384], P(('user', 'item', 'feat')), may hold values from -6 to 6
- tile_coords: int32 [64, 3], P(('user', 'item', 'feat')), may hold values from 0 to 7, as said below
- tile_live: int32 [64], P(('user', 'item', 'feat')), may hold values from 0 to 1, as said below
- side_matrix: bfloat16 [1024, 32768], P(('user', 'item'), 'feat'), may hold values from -6 to 6
- user_factor: bfloat16 [1024, 384], P('user'), may hold values from -2.1875 to 2.1875
- item_factor: bfloat16 [2048, 384], P('item'), may hold values from -2.1875 to 2.1875
- week_factor: bfloat16 [256, 384], replicated, may hold values from -2.1875 to 2.1875
- feat_factor: bfloat16 [384, 32768], P(('user', 'item'), 'feat'), may hold values from -0.59765625 to 0.59765625
Outputs:
- grad_user: float32 [1024, 384], P(('user', 'item', 'feat'))
- grad_item: float32 [2048, 384], P(None, ('user', 'item', 'feat'))
- grad_week: float32 [256, 384], P(None, ('user', 'item', 'feat'))
- grad_feat: float32 [384, 32768], P(('user', 'item'), 'feat')
The draws below stay inside these ranges and needn't reach their ends.
Inputs may be any that keep to these rules, and one draw needn't show every extreme that they name: `tile_coords`: column 0 is a user block, column 1 an item block, column 2 a week block. A slot on the device with user index u and item index i has its user block in u * 2 to u * 2 + 1 and its item block in i * 2 to i * 2 + 1. `tile_live`: on every device the live slots come first. Two devices whose feat indices differ only in the lowest bit hold 2 live slots together.
All inputs are finite; a program needn't handle non-finite values.
Results may differ from the reference program's by a relative error of at most 0.0014.
Values may be sent and summed in bfloat16 or wider, within the bound.
A program may use at most 128 MiB of HBM per device.

```python
import jax
import jax.numpy as jnp
from jax import lax

R = 384
BU = 256
BI = 256
BW = 64
UB_DEV = 2
IB_DEV = 2
NWB = 4
FEATS = 32768
TMAX = 2
USERS = 1024
ITEMS = 2048
WEEKS = 256
NT = 64


def draw_tile_live(key, part):
    device_count = NT // TMAX
    pair_count = device_count // 2
    first_count = jax.random.randint(jax.random.fold_in(key, 7), (pair_count,), 0, TMAX + 1)
    first_count = first_count.at[0].set(TMAX)
    per_device = jnp.stack([first_count, TMAX - first_count], axis=1).reshape(device_count)
    slot_ids = jnp.arange(TMAX, dtype=jnp.int32)
    return (slot_ids[None, :] < per_device[:, None]).astype(jnp.int32).reshape(NT)


def draw_tile_coords(key, part):
    device_count = NT // TMAX
    user_devices = USERS // (UB_DEV * BU)
    item_devices = ITEMS // (IB_DEV * BI)
    feat_devices = device_count // (user_devices * item_devices)
    device = jnp.arange(NT, dtype=jnp.int32) // TMAX
    user_index = device // (item_devices * feat_devices)
    item_index = device // feat_devices % item_devices
    subkeys = jax.random.split(jax.random.fold_in(key, 13), 3)
    user_offset = jax.random.randint(subkeys[0], (NT,), 0, UB_DEV)
    item_offset = jax.random.randint(subkeys[1], (NT,), 0, IB_DEV)
    week_block = jax.random.randint(subkeys[2], (NT,), 0, NWB)
    last_slot = NT - TMAX
    user_offset = user_offset.at[last_slot].set(UB_DEV - 1)
    item_offset = item_offset.at[last_slot].set(IB_DEV - 1)
    week_block = week_block.at[last_slot].set(NWB - 1)
    return jnp.stack([user_index * UB_DEV + user_offset, item_index * IB_DEV + item_offset, week_block], axis=1).astype(jnp.int32)


def steps_of(stream_key, shape, pieces, least, high):
    def one(axis_at, parts):
        heights = jax.random.uniform(jax.random.fold_in(jax.random.fold_in(stream_key, 6), axis_at), (parts,), jnp.float32, least / len(pieces), high / len(pieces))
        return jnp.repeat(jnp.exp(heights), shape[axis_at] // parts).reshape((-1,) + (1,) * (len(shape) - axis_at - 1))

    factor_of = one(*pieces[0])
    for cut in pieces[1:]:
        factor_of = factor_of * one(*cut)
    return factor_of


def bell_draw(key, extent, scale, most, cuts=(), held_as=jnp.bfloat16):
    array = scale * jax.random.normal(key, extent, jnp.float32)
    if cuts:
        array = array * steps_of(key, extent, cuts, -0.22, 0.18)
    return jnp.clip(array, -most, most).astype(held_as)


def setup_inputs(seed: int = 0) -> dict:
    seeds = jax.random.split(jax.random.key(seed), 9)
    return {
        "tensor_tiles": bell_draw(seeds[0], (NT, BU, BI * BW), 1.0, 6.0, ((0, 32),)),
        "tile_coords": draw_tile_coords(jax.random.fold_in(seeds[8], 71), 0),
        "tile_live": draw_tile_live(jax.random.fold_in(seeds[8], 71), 0),
        "side_matrix": bell_draw(seeds[3], (USERS, FEATS), 1.0, 6.0, ((0, 8), (1, 4))),
        "user_factor": bell_draw(seeds[4], (USERS, R), 0.37, 2.1875, ((0, 2),)),
        "item_factor": bell_draw(seeds[5], (ITEMS, R), 0.37, 2.1875, ((0, 4),)),
        "week_factor": bell_draw(seeds[6], (WEEKS, R), 0.37, 2.1875),
        "feat_factor": bell_draw(seeds[7], (R, FEATS), 0.1, 0.59765625, ((0, 8), (1, 4))),
    }


tensor_scale = 0.015625
side_scale = 0.03125


def tile_terms(block_tile, user_block, item_block, week_block):
    rows_item = item_block.shape[0]
    rows_week = week_block.shape[0]
    rank_width = user_block.shape[1]
    khatri = (item_block.astype(jnp.float32)[:, None, :] * week_block.astype(jnp.float32)[None, :, :]).reshape(rows_item * rows_week, rank_width).astype(jnp.bfloat16)
    predicted = lax.dot_general(user_block, khatri, (((1,), (1,)), ((), ())), preferred_element_type=jnp.float32)
    residual = (tensor_scale * (predicted - block_tile.astype(jnp.float32))).astype(jnp.bfloat16)
    user_term = jnp.dot(residual, khatri, preferred_element_type=jnp.float32)
    crossed = lax.dot_general(residual, user_block, (((0,), (0,)), ((), ())), preferred_element_type=jnp.float32).reshape(rows_item, rows_week, rank_width)
    item_term = jnp.sum(crossed * week_block.astype(jnp.float32)[None, :, :], axis=1)
    week_term = jnp.sum(crossed * item_block.astype(jnp.float32)[:, None, :], axis=0)
    return user_term, item_term, week_term


def add_rows(buffer, first_row, addend):
    current = lax.dynamic_slice_in_dim(buffer, first_row, addend.shape[0], 0)
    return lax.dynamic_update_slice_in_dim(buffer, current + addend, first_row, 0)


def reference(tensor_tiles, tile_coords, tile_live, side_matrix, user_factor, item_factor, week_factor, feat_factor):
    def one_slot(running, inputs):
        user_sum, item_sum, week_sum = running
        block_tile, coords, is_live = inputs
        user_start = (coords[0] * BU).astype(jnp.int32)
        item_start = (coords[1] * BI).astype(jnp.int32)
        week_start = (coords[2] * BW).astype(jnp.int32)

        def live_terms(unused):
            user_block = lax.dynamic_slice_in_dim(user_factor, user_start, BU, 0)
            item_block = lax.dynamic_slice_in_dim(item_factor, item_start, BI, 0)
            week_block = lax.dynamic_slice_in_dim(week_factor, week_start, BW, 0)
            return tile_terms(block_tile, user_block, item_block, week_block)

        def dead_terms(unused):
            return (jnp.zeros((BU, R), jnp.float32), jnp.zeros((BI, R), jnp.float32), jnp.zeros((BW, R), jnp.float32))

        user_term, item_term, week_term = lax.cond(is_live > 0, live_terms, dead_terms, 0)
        running = (add_rows(user_sum, user_start, user_term), add_rows(item_sum, item_start, item_term), add_rows(week_sum, week_start, week_term))
        return running, None

    running = (jnp.zeros((USERS, R), jnp.float32), jnp.zeros((ITEMS, R), jnp.float32), jnp.zeros((WEEKS, R), jnp.float32))
    running, unused = lax.scan(one_slot, running, (tensor_tiles, tile_coords, tile_live))
    tensor_user, grad_item, grad_week = running

    side_blocks = side_matrix.reshape(USERS // BU, BU, FEATS)
    user_blocks = user_factor.reshape(USERS // BU, BU, R)

    def side_step(feat_sum, inputs):
        side_rows, user_rows = inputs
        predicted = jnp.dot(user_rows, feat_factor, preferred_element_type=jnp.float32)
        side_resid = (side_scale * (predicted - side_rows.astype(jnp.float32))).astype(jnp.bfloat16)
        side_user = lax.dot_general(side_resid, feat_factor, (((1,), (1,)), ((), ())), preferred_element_type=jnp.float32)
        feat_sum = feat_sum + lax.dot_general(user_rows, side_resid, (((0,), (0,)), ((), ())), preferred_element_type=jnp.float32)
        return feat_sum, side_user

    grad_feat, side_users = lax.scan(side_step, jnp.zeros((R, FEATS), jnp.float32), (side_blocks, user_blocks))
    grad_user = tensor_user + side_users.reshape(USERS, R)
    return (grad_user, grad_item, grad_week, grad_feat)
```

```python
import jax
import jax.numpy as jnp
from jax import lax
from jax.experimental import pallas as pl
from jax.experimental.pallas import tpu as pltpu
from jax.sharding import PartitionSpec as P

BU = 256
BI = 256
BW = 64
ITEMS_STEP = 16

tensor_scale = 0.015625
side_scale = 0.03125


def tile_kernel(starts, live, tile, user, item, week, user_sum, item_sum, week_sum):
    slot = pl.program_id(0)
    step = pl.program_id(1)

    @pl.when((slot == 0) & (step == 0))
    def _():
        user_sum[...] = jnp.zeros_like(user_sum)
        item_sum[...] = jnp.zeros_like(item_sum)
        week_sum[...] = jnp.zeros_like(week_sum)

    @pl.when(live[slot] > 0)
    def _():
        user_rows = pl.ds(pl.multiple_of(starts[slot, 0], BU), BU)
        item_rows = pl.ds(
            pl.multiple_of(starts[slot, 1] + step * ITEMS_STEP, ITEMS_STEP), ITEMS_STEP
        )
        week_rows = pl.ds(pl.multiple_of(starts[slot, 2], BW), BW)
        users = user[user_rows, :]
        items = item[item_rows, :].astype(jnp.float32)
        weeks = week[week_rows, :].astype(jnp.float32)
        rank = users.shape[1]
        khatri = (
            (items[:, None, :] * weeks[None, :, :])
            .reshape(ITEMS_STEP * BW, rank)
            .astype(jnp.bfloat16)
        )
        predicted = lax.dot_general(
            users, khatri, (((1,), (1,)), ((), ())), preferred_element_type=jnp.float32
        )
        residual = (tensor_scale * (predicted - tile[0].astype(jnp.float32))).astype(
            jnp.bfloat16
        )
        user_sum[user_rows, :] += jnp.dot(residual, khatri, preferred_element_type=jnp.float32)
        crossed = lax.dot_general(
            residual, users, (((0,), (0,)), ((), ())), preferred_element_type=jnp.float32
        ).reshape(ITEMS_STEP, BW, rank)
        item_sum[item_rows, :] += jnp.sum(crossed * weeks[None, :, :], axis=1)
        week_sum[week_rows, :] += jnp.sum(crossed * items[:, None, :], axis=0)


def tile_sums(tensor_tiles, tile_coords, tile_live, user_factor, item_factor, week_factor):
    slots, _, width = tensor_tiles.shape
    rank = user_factor.shape[1]
    steps = BI // ITEMS_STEP
    starts = jnp.stack(
        [
            lax.rem(tile_coords[:, 0] * BU, user_factor.shape[0]),
            lax.rem(tile_coords[:, 1] * BI, item_factor.shape[0]),
            tile_coords[:, 2] * BW,
        ],
        axis=1,
    )

    def tile_map(s, j, starts, live):
        count = live[0]
        for k in range(1, slots):
            count += live[k]
        dead = s >= count
        return (
            jnp.where(dead, jnp.maximum(count - 1, 0), s),
            0,
            jnp.where(dead, jnp.where(count > 0, steps - 1, 0), j),
        )

    whole = lambda a: pl.BlockSpec(a.shape, lambda s, j, *_: (0, 0))
    outs = [
        jax.ShapeDtypeStruct(a.shape, jnp.float32)
        for a in (user_factor, item_factor, week_factor)
    ]
    return pl.pallas_call(
        tile_kernel,
        grid_spec=pltpu.PrefetchScalarGridSpec(
            num_scalar_prefetch=2,
            grid=(slots, steps),
            in_specs=[
                pl.BlockSpec((1, BU, ITEMS_STEP * BW), tile_map),
                whole(user_factor),
                whole(item_factor),
                whole(week_factor),
            ],
            out_specs=[whole(a) for a in outs],
        ),
        out_shape=outs,
        compiler_params=pltpu.CompilerParams(
            dimension_semantics=("arbitrary", "arbitrary"),
            vmem_limit_bytes=40 * 1024 * 1024,
        ),
        cost_estimate=pl.CostEstimate(
            flops=slots * 6 * BU * width * rank,
            bytes_accessed=slots * 2 * BU * width,
            transcendentals=0,
        ),
        name="tile_sums",
    )(starts, tile_live, tensor_tiles, user_factor, item_factor, week_factor)


def gather_rows(block, axis):
    count = lax.axis_size(axis)
    me = lax.axis_index(axis)
    rows = block.shape[0]
    whole = jnp.zeros((count * rows,) + block.shape[1:], block.dtype)
    for shift in range(count):
        piece = block
        if shift:
            piece = lax.ppermute(
                block, axis, [(k, (k + shift) % count) for k in range(count)]
            )
        whole = lax.dynamic_update_slice_in_dim(
            whole, piece, lax.rem(me - shift + count, count) * rows, 0
        )
    return whole


def exchange(blocks, axes):
    return lax.all_to_all(blocks, axes, split_axis=0, concat_axis=0, tiled=True)


def local(
    tensor_tiles,
    tile_coords,
    tile_live,
    side_matrix,
    user_factor,
    item_factor,
    week_factor,
    feat_factor,
):
    user_rows, rank = user_factor.shape
    item_rows = item_factor.shape[0]
    week_rows = week_factor.shape[0]
    n_user = lax.axis_size("user")
    n_item = lax.axis_size("item")
    n_feat = lax.axis_size("feat")
    own = rank // (n_user * n_item * n_feat)
    user_base = lax.axis_index("user") * user_rows

    factor_cols = lax.all_to_all(
        feat_factor, ("user", "item"), split_axis=1, concat_axis=0, tiled=True
    )
    side_cols = lax.all_to_all(
        side_matrix, ("user", "item"), split_axis=1, concat_axis=0, tiled=True
    )
    all_users = gather_rows(user_factor, "user")

    user_sum, item_sum, week_sum = tile_sums(
        tensor_tiles, tile_coords, tile_live, user_factor, item_factor, week_factor
    )

    both = jnp.concatenate([item_sum, week_sum], axis=0).T
    both = both.reshape(n_user, n_item, n_feat, own, item_rows + week_rows)
    both = both.transpose(0, 2, 1, 3, 4).reshape(
        n_user * n_feat, n_item * own, item_rows + week_rows
    )
    both = jnp.sum(exchange(both, ("user", "feat")), axis=0)
    both = exchange(both.reshape(n_item, own, item_rows + week_rows), "item")
    grad_item = both[:, :, :item_rows].transpose(0, 2, 1).reshape(n_item * item_rows, own)
    grad_week = jnp.sum(both[:, :, item_rows:], axis=0).T

    predicted = jnp.dot(all_users, factor_cols, preferred_element_type=jnp.float32)
    side_resid = (side_scale * (predicted - side_cols.astype(jnp.float32))).astype(jnp.bfloat16)
    feat_cols = lax.dot_general(
        all_users, side_resid, (((0,), (0,)), ((), ())), preferred_element_type=jnp.float32
    )
    grad_feat = lax.all_to_all(feat_cols, ("user", "item"), split_axis=0, concat_axis=1, tiled=True)
    side_user = lax.dot_general(
        side_resid, factor_cols, (((1,), (1,)), ((), ())), preferred_element_type=jnp.float32
    )
    mine = lax.dynamic_slice_in_dim(side_user, user_base, user_rows, 0)
    user_total = lax.dynamic_update_slice_in_dim(side_user, mine + user_sum, user_base, 0)
    rows = user_total.shape[0] // (n_user * n_item * n_feat)
    by_feat = user_total.reshape(n_user * n_item, n_feat, rows, rank).transpose(1, 0, 2, 3)
    by_feat = jnp.sum(exchange(by_feat, "feat"), axis=0)
    grad_user = jnp.sum(exchange(by_feat, ("user", "item")), axis=0)
    return (grad_user, grad_item, grad_week, grad_feat)


def solution(mesh):
    return jax.shard_map(
        local,
        mesh=mesh,
        in_specs=(
            P(("user", "item", "feat"), None, None),
            P(("user", "item", "feat"), None),
            P(("user", "item", "feat")),
            P(("user", "item"), "feat"),
            P("user", None),
            P("item", None),
            P(),
            P(("user", "item"), "feat"),
        ),
        out_specs=(
            P(("user", "item", "feat"), None),
            P(None, ("user", "item", "feat")),
            P(None, ("user", "item", "feat")),
            P(("user", "item"), "feat"),
        ),
        check_vma=False,
    )
```

```python
import jax
import jax.numpy as jnp
from jax import lax
from jax.experimental import pallas as pl
from jax.experimental.pallas import tpu as pltpu
from jax.sharding import PartitionSpec as P

BU = 256
BI = 256
BW = 64
ITEMS_STEP = 16

tensor_scale = 0.015625
side_scale = 0.03125


def tile_kernel(starts, live, tile, user, item, week, user_sum, item_sum, week_sum):
    slot = pl.program_id(0)
    step = pl.program_id(1)

    @pl.when((slot == 0) & (step == 0))
    def _():
        user_sum[...] = jnp.zeros_like(user_sum)
        item_sum[...] = jnp.zeros_like(item_sum)
        week_sum[...] = jnp.zeros_like(week_sum)

    @pl.when(live[slot] > 0)
    def _():
        user_rows = pl.ds(pl.multiple_of(starts[slot, 0], BU), BU)
        item_rows = pl.ds(
            pl.multiple_of(starts[slot, 1] + step * ITEMS_STEP, ITEMS_STEP), ITEMS_STEP
        )
        week_rows = pl.ds(pl.multiple_of(starts[slot, 2], BW), BW)
        users = user[user_rows, :]
        items = item[item_rows, :].astype(jnp.float32)
        weeks = week[week_rows, :].astype(jnp.float32)
        rank = users.shape[1]
        khatri = (
            (items[:, None, :] * weeks[None, :, :])
            .reshape(ITEMS_STEP * BW, rank)
            .astype(jnp.bfloat16)
        )
        predicted = lax.dot_general(
            users, khatri, (((1,), (1,)), ((), ())), preferred_element_type=jnp.float32
        )
        residual = (tensor_scale * (predicted - tile[0].astype(jnp.float32))).astype(
            jnp.bfloat16
        )
        user_sum[user_rows, :] += jnp.dot(residual, khatri, preferred_element_type=jnp.float32)
        crossed = lax.dot_general(
            residual, users, (((0,), (0,)), ((), ())), preferred_element_type=jnp.float32
        ).reshape(ITEMS_STEP, BW, rank)
        item_sum[item_rows, :] += jnp.sum(crossed * weeks[None, :, :], axis=1)
        week_sum[week_rows, :] += jnp.sum(crossed * items[:, None, :], axis=0)


def tile_sums(tensor_tiles, tile_coords, tile_live, user_factor, item_factor, week_factor):
    slots, _, width = tensor_tiles.shape
    rank = user_factor.shape[1]
    steps = BI // ITEMS_STEP
    starts = jnp.stack(
        [
            lax.rem(tile_coords[:, 0] * BU, user_factor.shape[0]),
            lax.rem(tile_coords[:, 1] * BI, item_factor.shape[0]),
            tile_coords[:, 2] * BW,
        ],
        axis=1,
    )

    def tile_map(s, j, starts, live):
        count = live[0]
        for k in range(1, slots):
            count += live[k]
        dead = s >= count
        return (
            jnp.where(dead, jnp.maximum(count - 1, 0), s),
            0,
            jnp.where(dead, jnp.where(count > 0, steps - 1, 0), j),
        )

    whole = lambda a: pl.BlockSpec(a.shape, lambda s, j, *_: (0, 0))
    outs = [
        jax.ShapeDtypeStruct(a.shape, jnp.float32)
        for a in (user_factor, item_factor, week_factor)
    ]
    return pl.pallas_call(
        tile_kernel,
        grid_spec=pltpu.PrefetchScalarGridSpec(
            num_scalar_prefetch=2,
            grid=(slots, steps),
            in_specs=[
                pl.BlockSpec((1, BU, ITEMS_STEP * BW), tile_map),
                whole(user_factor),
                whole(item_factor),
                whole(week_factor),
            ],
            out_specs=[whole(a) for a in outs],
        ),
        out_shape=outs,
        compiler_params=pltpu.CompilerParams(
            dimension_semantics=("arbitrary", "arbitrary"),
            vmem_limit_bytes=40 * 1024 * 1024,
        ),
        cost_estimate=pl.CostEstimate(
            flops=slots * 6 * BU * width * rank,
            bytes_accessed=slots * 2 * BU * width,
            transcendentals=0,
        ),
        name="tile_sums",
    )(starts, tile_live, tensor_tiles, user_factor, item_factor, week_factor)


def gather_rows(block, axis):
    count = lax.axis_size(axis)
    me = lax.axis_index(axis)
    rows = block.shape[0]
    whole = jnp.zeros((count * rows,) + block.shape[1:], block.dtype)
    for shift in range(count):
        piece = block
        if shift:
            piece = lax.ppermute(
                block, axis, [(k, (k + shift) % count) for k in range(count)]
            )
        whole = lax.dynamic_update_slice_in_dim(
            whole, piece, lax.rem(me - shift + count, count) * rows, 0
        )
    return whole


def peer(axes, shift):
    size = 1
    me = 0
    for axis in axes:
        size *= lax.axis_size(axis)
        me = me * lax.axis_size(axis) + lax.axis_index(axis)
    place = lax.rem(me + shift, size)
    left = place
    device = {}
    for axis in reversed(axes):
        device[axis] = lax.rem(left, lax.axis_size(axis))
        left = left // lax.axis_size(axis)
    return device, place


def tail_kernel(
    feat_in, user_in, both_in,
    feat_out, user_out, item_out, week_out,
    user_got, user_mid, user_last, both_got, both_mid, both_last,
    own_sem, feat_sems, user_sems, last_sems, both_sems, item_sems,
):
    columns = ("user", "item")
    sums = ("user", "feat")
    n_columns = feat_in.shape[0]
    n_feat = user_in.shape[0]
    n_sums = both_in.shape[0]
    n_item = both_mid.shape[0]
    me_columns = peer(columns, 0)[1]
    me_feat = lax.axis_index("feat")
    me_sums = peer(sums, 0)[1]
    me_item = lax.axis_index("item")

    barrier = pltpu.get_barrier_semaphore()
    for axes, count in ((columns, n_columns), (sums, n_sums)):
        for shift in range(1, count):
            pl.semaphore_signal(
                barrier, inc=1, device_id=peer(axes, shift)[0],
                device_id_type=pl.DeviceIdType.MESH,
            )
    pl.semaphore_wait(barrier, n_columns + n_sums - 2)

    def send(src, dst, sems, shift, device):
        copy = pltpu.make_async_remote_copy(
            src_ref=src, dst_ref=dst, send_sem=sems.at[0, shift - 1],
            recv_sem=sems.at[1, shift - 1], device_id=device,
            device_id_type=pl.DeviceIdType.MESH,
        )
        copy.start()
        return copy

    both_copies = []
    for shift in range(1, n_sums):
        device, place = peer(sums, shift)
        both_copies.append(
            send(both_in.at[place], both_got.at[shift - 1], both_sems, shift, device)
        )
    user_copies = []
    for shift in range(1, n_feat):
        device, place = peer(("feat",), shift)
        user_copies.append(
            send(user_in.at[place], user_got.at[shift - 1], user_sems, shift, device)
        )
    width = feat_in.shape[2]
    mine = pl.ds(pl.multiple_of(me_columns * width, width), width)
    feat_copies = []
    for shift in range(1, n_columns):
        device, place = peer(columns, shift)
        feat_copies.append(
            send(feat_in.at[place], feat_out.at[:, mine], feat_sems, shift, device)
        )
    own = pltpu.make_async_copy(feat_in.at[me_columns], feat_out.at[:, mine], own_sem)
    own.start()

    for copy in both_copies:
        copy.wait_recv()
    total = both_in[me_sums]
    for k in range(n_sums - 1):
        total += both_got[k]
    both_mid[...] = total
    item_copies = []
    for shift in range(1, n_item):
        device, place = peer(("item",), shift)
        item_copies.append(
            send(both_mid.at[place], both_last.at[shift - 1], item_sems, shift, device)
        )

    for copy in user_copies:
        copy.wait_recv()
    total = user_in[me_feat]
    for k in range(n_feat - 1):
        total += user_got[k]
    user_mid[...] = total
    last_copies = []
    for shift in range(1, n_columns):
        device, place = peer(columns, shift)
        last_copies.append(
            send(user_mid.at[place], user_last.at[shift - 1], last_sems, shift, device)
        )

    item_rows = item_out.shape[2]
    for copy in item_copies:
        copy.wait_recv()
    block = both_mid[me_item]
    item_out[me_item] = block[:, :item_rows]
    week = block[:, item_rows:]
    for shift in range(1, n_item):
        block = both_last[shift - 1]
        item_out[lax.rem(me_item - shift + n_item, n_item)] = block[:, :item_rows]
        week += block[:, item_rows:]
    week_out[...] = week

    for copy in last_copies:
        copy.wait_recv()
    total = user_mid[me_columns]
    for k in range(n_columns - 1):
        total += user_last[k]
    user_out[...] = total

    own.wait()
    for copy in feat_copies:
        copy.wait_recv()
    for copy in both_copies + user_copies + feat_copies + item_copies + last_copies:
        copy.wait_send()


def tail(feat_in, user_in, both_in, item_rows):
    n_columns, own_ranks, width = feat_in.shape
    n_feat, _, rows, rank = user_in.shape
    n_sums, n_item, own, length = both_in.shape
    f32 = jnp.float32
    vmem = pl.BlockSpec(memory_space=pltpu.VMEM)
    pairs = lambda count: pltpu.SemaphoreType.DMA((2, count - 1))
    return pl.pallas_call(
        tail_kernel,
        in_specs=[vmem] * 3,
        out_specs=[vmem] * 4,
        out_shape=[
            jax.ShapeDtypeStruct((own_ranks, n_columns * width), f32),
            jax.ShapeDtypeStruct((rows, rank), f32),
            jax.ShapeDtypeStruct((n_item, own, item_rows), f32),
            jax.ShapeDtypeStruct((own, length - item_rows), f32),
        ],
        scratch_shapes=[
            pltpu.VMEM((n_feat - 1, n_columns, rows, rank), f32),
            pltpu.VMEM((n_columns, rows, rank), f32),
            pltpu.VMEM((n_columns - 1, rows, rank), f32),
            pltpu.VMEM((n_sums - 1, n_item, own, length), f32),
            pltpu.VMEM((n_item, own, length), f32),
            pltpu.VMEM((n_item - 1, own, length), f32),
            pltpu.SemaphoreType.DMA,
            pairs(n_columns),
            pairs(n_feat),
            pairs(n_columns),
            pairs(n_sums),
            pairs(n_item),
        ],
        compiler_params=pltpu.CompilerParams(
            collective_id=0, has_side_effects=True, vmem_limit_bytes=48 * 1024 * 1024
        ),
        name="tail_exchange",
    )(feat_in, user_in, both_in)


def local(
    tensor_tiles,
    tile_coords,
    tile_live,
    side_matrix,
    user_factor,
    item_factor,
    week_factor,
    feat_factor,
):
    user_rows, rank = user_factor.shape
    item_rows = item_factor.shape[0]
    week_rows = week_factor.shape[0]
    n_user = lax.axis_size("user")
    n_item = lax.axis_size("item")
    n_feat = lax.axis_size("feat")
    own = rank // (n_user * n_item * n_feat)
    user_base = lax.axis_index("user") * user_rows

    side_rows = side_matrix.shape[0]
    n_columns = n_user * n_item
    sent = jnp.concatenate([side_matrix, feat_factor], axis=0)
    got = lax.all_to_all(sent, ("user", "item"), split_axis=1, concat_axis=0, tiled=True)
    got = got.reshape(n_columns, sent.shape[0], got.shape[1])
    side_cols = got[:, :side_rows].reshape(n_columns * side_rows, got.shape[2])
    factor_cols = got[:, side_rows:].reshape(rank, got.shape[2])
    all_users = gather_rows(user_factor, "user")

    user_sum, item_sum, week_sum = tile_sums(
        tensor_tiles, tile_coords, tile_live, user_factor, item_factor, week_factor
    )

    both = jnp.concatenate([item_sum, week_sum], axis=0).T
    both = both.reshape(n_user, n_item, n_feat, own, item_rows + week_rows)
    both = both.transpose(0, 2, 1, 3, 4).reshape(
        n_user * n_feat, n_item, own, item_rows + week_rows
    )

    predicted = jnp.dot(all_users, factor_cols, preferred_element_type=jnp.float32)
    side_resid = (side_scale * (predicted - side_cols.astype(jnp.float32))).astype(jnp.bfloat16)
    feat_cols = lax.dot_general(
        all_users, side_resid, (((0,), (0,)), ((), ())), preferred_element_type=jnp.float32
    )
    feat_cols = feat_cols.reshape(n_columns, rank // n_columns, feat_cols.shape[1])
    side_user = lax.dot_general(
        side_resid, factor_cols, (((1,), (1,)), ((), ())), preferred_element_type=jnp.float32
    )
    mine = lax.dynamic_slice_in_dim(side_user, user_base, user_rows, 0)
    user_total = lax.dynamic_update_slice_in_dim(side_user, mine + user_sum, user_base, 0)
    rows = user_total.shape[0] // (n_user * n_item * n_feat)
    by_feat = user_total.reshape(n_user * n_item, n_feat, rows, rank).transpose(1, 0, 2, 3)
    grad_feat, grad_user, by_item, by_week = tail(feat_cols, by_feat, both, item_rows)
    grad_item = by_item.transpose(0, 2, 1).reshape(n_item * item_rows, own)
    grad_week = by_week.T
    return (grad_user, grad_item, grad_week, grad_feat)


def solution(mesh):
    return jax.shard_map(
        local,
        mesh=mesh,
        in_specs=(
            P(("user", "item", "feat"), None, None),
            P(("user", "item", "feat"), None),
            P(("user", "item", "feat")),
            P(("user", "item"), "feat"),
            P("user", None),
            P("item", None),
            P(),
            P(("user", "item"), "feat"),
        ),
        out_specs=(
            P(("user", "item", "feat"), None),
            P(None, ("user", "item", "feat")),
            P(None, ("user", "item", "feat")),
            P(("user", "item"), "feat"),
        ),
        check_vma=False,
    )
```

```python
import jax
import jax.numpy as jnp
from jax import lax
from jax.experimental import pallas as pl
from jax.experimental.pallas import tpu as pltpu
from jax.sharding import PartitionSpec as P

BU = 256
BI = 256
BW = 64
ITEMS_STEP = 16

tensor_scale = 0.015625
side_scale = 0.03125


def tile_kernel(starts, live, tile, user, item, week, user_sum, item_sum, week_sum):
    slot = pl.program_id(0)
    step = pl.program_id(1)

    @pl.when((slot == 0) & (step == 0))
    def _():
        user_sum[...] = jnp.zeros_like(user_sum)
        item_sum[...] = jnp.zeros_like(item_sum)
        week_sum[...] = jnp.zeros_like(week_sum)

    @pl.when(live[slot] > 0)
    def _():
        user_rows = pl.ds(pl.multiple_of(starts[slot, 0], BU), BU)
        item_rows = pl.ds(
            pl.multiple_of(starts[slot, 1] + step * ITEMS_STEP, ITEMS_STEP), ITEMS_STEP
        )
        week_rows = pl.ds(pl.multiple_of(starts[slot, 2], BW), BW)
        users = user[user_rows, :]
        items = item[item_rows, :].astype(jnp.float32)
        weeks = week[week_rows, :].astype(jnp.float32)
        rank = users.shape[1]
        khatri = (
            (items[:, None, :] * weeks[None, :, :])
            .reshape(ITEMS_STEP * BW, rank)
            .astype(jnp.bfloat16)
        )
        predicted = lax.dot_general(
            users, khatri, (((1,), (1,)), ((), ())), preferred_element_type=jnp.float32
        )
        residual = (tensor_scale * (predicted - tile[0].astype(jnp.float32))).astype(
            jnp.bfloat16
        )
        user_sum[user_rows, :] += jnp.dot(residual, khatri, preferred_element_type=jnp.float32)
        crossed = lax.dot_general(
            residual, users, (((0,), (0,)), ((), ())), preferred_element_type=jnp.float32
        ).reshape(ITEMS_STEP, BW, rank)
        item_sum[item_rows, :] += jnp.sum(crossed * weeks[None, :, :], axis=1)
        week_sum[week_rows, :] += jnp.sum(crossed * items[:, None, :], axis=0)


def tile_sums(tensor_tiles, tile_coords, tile_live, user_factor, item_factor, week_factor):
    slots, _, width = tensor_tiles.shape
    rank = user_factor.shape[1]
    steps = BI // ITEMS_STEP
    starts = jnp.stack(
        [
            lax.rem(tile_coords[:, 0] * BU, user_factor.shape[0]),
            lax.rem(tile_coords[:, 1] * BI, item_factor.shape[0]),
            tile_coords[:, 2] * BW,
        ],
        axis=1,
    )

    def tile_map(s, j, starts, live):
        count = live[0]
        for k in range(1, slots):
            count += live[k]
        dead = s >= count
        return (
            jnp.where(dead, jnp.maximum(count - 1, 0), s),
            0,
            jnp.where(dead, jnp.where(count > 0, steps - 1, 0), j),
        )

    whole = lambda a: pl.BlockSpec(a.shape, lambda s, j, *_: (0, 0))
    outs = [
        jax.ShapeDtypeStruct(a.shape, jnp.float32)
        for a in (user_factor, item_factor, week_factor)
    ]
    return pl.pallas_call(
        tile_kernel,
        grid_spec=pltpu.PrefetchScalarGridSpec(
            num_scalar_prefetch=2,
            grid=(slots, steps),
            in_specs=[
                pl.BlockSpec((1, BU, ITEMS_STEP * BW), tile_map),
                whole(user_factor),
                whole(item_factor),
                whole(week_factor),
            ],
            out_specs=[whole(a) for a in outs],
        ),
        out_shape=outs,
        compiler_params=pltpu.CompilerParams(
            dimension_semantics=("arbitrary", "arbitrary"),
            vmem_limit_bytes=40 * 1024 * 1024,
        ),
        cost_estimate=pl.CostEstimate(
            flops=slots * 6 * BU * width * rank,
            bytes_accessed=slots * 2 * BU * width,
            transcendentals=0,
        ),
        name="tile_sums",
    )(starts, tile_live, tensor_tiles, user_factor, item_factor, week_factor)


def gather_rows(block, axis):
    count = lax.axis_size(axis)
    me = lax.axis_index(axis)
    rows = block.shape[0]
    whole = jnp.zeros((count * rows,) + block.shape[1:], block.dtype)
    for shift in range(count):
        piece = block
        if shift:
            piece = lax.ppermute(
                block, axis, [(k, (k + shift) % count) for k in range(count)]
            )
        whole = lax.dynamic_update_slice_in_dim(
            whole, piece, lax.rem(me - shift + count, count) * rows, 0
        )
    return whole


def peer(axes, shift):
    size = 1
    me = 0
    for axis in axes:
        size *= lax.axis_size(axis)
        me = me * lax.axis_size(axis) + lax.axis_index(axis)
    place = lax.rem(me + shift, size)
    left = place
    device = {}
    for axis in reversed(axes):
        device[axis] = lax.rem(left, lax.axis_size(axis))
        left = left // lax.axis_size(axis)
    return device, place


def greet(groups):
    barrier = pltpu.get_barrier_semaphore()
    expected = 0
    for axes, count in groups:
        for shift in range(1, count):
            pl.semaphore_signal(
                barrier, inc=1, device_id=peer(axes, shift)[0],
                device_id_type=pl.DeviceIdType.MESH,
            )
        expected += count - 1
    pl.semaphore_wait(barrier, expected)


def send(src, dst, sems, shift, device):
    copy = pltpu.make_async_remote_copy(
        src_ref=src, dst_ref=dst, send_sem=sems.at[0, shift - 1],
        recv_sem=sems.at[1, shift - 1], device_id=device,
        device_id_type=pl.DeviceIdType.MESH,
    )
    copy.start()
    return copy


def item_kernel(
    both_in, item_out, week_out, both_got, both_mid, both_last, both_sems, item_sems
):
    sums = ("user", "feat")
    n_sums = both_in.shape[0]
    n_item = both_mid.shape[0]
    me_sums = peer(sums, 0)[1]
    me_item = lax.axis_index("item")
    greet(((sums, n_sums), (("item",), n_item)))

    both_copies = []
    for shift in range(1, n_sums):
        device, place = peer(sums, shift)
        both_copies.append(
            send(both_in.at[place], both_got.at[shift - 1], both_sems, shift, device)
        )
    for copy in both_copies:
        copy.wait_recv()
    total = both_in[me_sums]
    for k in range(n_sums - 1):
        total += both_got[k]
    both_mid[...] = total
    item_copies = []
    for shift in range(1, n_item):
        device, place = peer(("item",), shift)
        item_copies.append(
            send(both_mid.at[place], both_last.at[shift - 1], item_sems, shift, device)
        )
    item_rows = item_out.shape[2]
    for copy in item_copies:
        copy.wait_recv()
    block = both_mid[me_item]
    item_out[me_item] = block[:, :item_rows]
    week = block[:, item_rows:]
    for shift in range(1, n_item):
        block = both_last[shift - 1]
        item_out[lax.rem(me_item - shift + n_item, n_item)] = block[:, :item_rows]
        week += block[:, item_rows:]
    week_out[...] = week
    for copy in both_copies + item_copies:
        copy.wait_send()


def tail_kernel(
    scale_in, user_in, scale_out, user_out,
    user_got, user_mid, user_last, own_sem, scale_sems, user_sems, last_sems,
):
    columns = ("user", "item")
    n_columns = scale_out.shape[0]
    n_feat = user_in.shape[0]
    me_columns = peer(columns, 0)[1]
    me_feat = lax.axis_index("feat")
    greet(((columns, n_columns), (("feat",), n_feat)))

    user_copies = []
    for shift in range(1, n_feat):
        device, place = peer(("feat",), shift)
        user_copies.append(
            send(user_in.at[place], user_got.at[shift - 1], user_sems, shift, device)
        )
    scale_copies = []
    for shift in range(1, n_columns):
        device, place = peer(columns, shift)
        scale_copies.append(
            send(scale_in, scale_out.at[me_columns], scale_sems, shift, device)
        )
    own = pltpu.make_async_copy(scale_in, scale_out.at[me_columns], own_sem)
    own.start()

    for copy in user_copies:
        copy.wait_recv()
    total = user_in[me_feat]
    for k in range(n_feat - 1):
        total += user_got[k]
    user_mid[...] = total
    last_copies = []
    for shift in range(1, n_columns):
        device, place = peer(columns, shift)
        last_copies.append(
            send(user_mid.at[place], user_last.at[shift - 1], last_sems, shift, device)
        )
    for copy in last_copies:
        copy.wait_recv()
    total = user_mid[me_columns]
    for k in range(n_columns - 1):
        total += user_last[k]
    user_out[...] = total

    own.wait()
    for copy in scale_copies:
        copy.wait_recv()
    for copy in user_copies + scale_copies + last_copies:
        copy.wait_send()


def pair_sems(count):
    return pltpu.SemaphoreType.DMA((2, count - 1))


def item_exchange(both_in, item_rows):
    n_sums, n_item, own, length = both_in.shape
    f32 = jnp.float32
    vmem = pl.BlockSpec(memory_space=pltpu.VMEM)
    return pl.pallas_call(
        item_kernel,
        in_specs=[vmem],
        out_specs=[vmem] * 2,
        out_shape=[
            jax.ShapeDtypeStruct((n_item, own, item_rows), f32),
            jax.ShapeDtypeStruct((own, length - item_rows), f32),
        ],
        scratch_shapes=[
            pltpu.VMEM((n_sums - 1, n_item, own, length), f32),
            pltpu.VMEM((n_item, own, length), f32),
            pltpu.VMEM((n_item - 1, own, length), f32),
            pair_sems(n_sums),
            pair_sems(n_item),
        ],
        compiler_params=pltpu.CompilerParams(
            collective_id=1, has_side_effects=True, vmem_limit_bytes=32 * 1024 * 1024
        ),
        cost_estimate=pl.CostEstimate(
            flops=10**9, bytes_accessed=40 * 10**6, transcendentals=0
        ),
        name="item_exchange",
    )(both_in)


def tail(scale_in, user_in):
    n_feat, n_columns, rows, rank = user_in.shape
    f32 = jnp.float32
    vmem = pl.BlockSpec(memory_space=pltpu.VMEM)
    return pl.pallas_call(
        tail_kernel,
        in_specs=[vmem] * 2,
        out_specs=[vmem] * 2,
        out_shape=[
            jax.ShapeDtypeStruct((n_columns,) + scale_in.shape, f32),
            jax.ShapeDtypeStruct((rows, rank), f32),
        ],
        scratch_shapes=[
            pltpu.VMEM((n_feat - 1, n_columns, rows, rank), f32),
            pltpu.VMEM((n_columns, rows, rank), f32),
            pltpu.VMEM((n_columns - 1, rows, rank), f32),
            pltpu.SemaphoreType.DMA,
            pair_sems(n_columns),
            pair_sems(n_feat),
            pair_sems(n_columns),
        ],
        compiler_params=pltpu.CompilerParams(
            collective_id=0, has_side_effects=True, vmem_limit_bytes=48 * 1024 * 1024
        ),
        cost_estimate=pl.CostEstimate(
            flops=10**9, bytes_accessed=80 * 10**6, transcendentals=0
        ),
        name="tail_exchange",
    )(scale_in, user_in)


def exchange(blocks, axes):
    return lax.all_to_all(blocks, axes, split_axis=0, concat_axis=0, tiled=True)


def local(
    tensor_tiles,
    tile_coords,
    tile_live,
    side_matrix,
    user_factor,
    item_factor,
    week_factor,
    feat_factor,
):
    user_rows, rank = user_factor.shape
    item_rows = item_factor.shape[0]
    week_rows = week_factor.shape[0]
    n_user = lax.axis_size("user")
    n_item = lax.axis_size("item")
    n_feat = lax.axis_size("feat")
    own = rank // (n_user * n_item * n_feat)
    user_base = lax.axis_index("user") * user_rows

    side_rows = side_matrix.shape[0]
    n_columns = n_user * n_item
    sent = jnp.concatenate([side_matrix, feat_factor], axis=0)
    got = lax.all_to_all(sent, ("user", "item"), split_axis=1, concat_axis=0, tiled=True)
    all_users = gather_rows(user_factor, "user")

    user_sum, item_sum, week_sum = tile_sums(
        tensor_tiles, tile_coords, tile_live, user_factor, item_factor, week_factor
    )

    both = jnp.concatenate([item_sum, week_sum], axis=0).T
    both = both.reshape(n_user, n_item, n_feat, own, item_rows + week_rows)
    both = both.transpose(0, 2, 1, 3, 4).reshape(
        n_user * n_feat, n_item, own, item_rows + week_rows
    )
    by_item, by_week = item_exchange(both, item_rows)
    got, by_item, by_week, user_sum = lax.optimization_barrier((got, by_item, by_week, user_sum))
    got = got.reshape(n_columns, sent.shape[0], got.shape[1])
    side_cols = got[:, :side_rows].reshape(n_columns * side_rows, got.shape[2])
    factor_cols = got[:, side_rows:].reshape(rank, got.shape[2])
    grad_item = by_item.transpose(0, 2, 1).reshape(n_item * item_rows, own)
    grad_week = by_week.T

    predicted = jnp.dot(all_users, factor_cols, preferred_element_type=jnp.float32)
    side_resid = (side_scale * (predicted - side_cols.astype(jnp.float32))).astype(jnp.bfloat16)
    feat_cols = lax.dot_general(
        all_users, side_resid, (((0,), (0,)), ((), ())), preferred_element_type=jnp.float32
    )
    width = feat_cols.shape[1]
    scale = jnp.maximum(jnp.max(jnp.abs(feat_cols)), 1e-30) / 16384.0
    own_ranks = rank // n_columns
    coded = (feat_cols * (1.0 / scale)).astype(jnp.float16)
    coded = exchange(coded.reshape(n_columns, own_ranks, width), ("user", "item"))
    side_user = lax.dot_general(
        side_resid, factor_cols, (((1,), (1,)), ((), ())), preferred_element_type=jnp.float32
    )
    mine = lax.dynamic_slice_in_dim(side_user, user_base, user_rows, 0)
    user_total = lax.dynamic_update_slice_in_dim(side_user, mine + user_sum, user_base, 0)
    rows = user_total.shape[0] // (n_user * n_item * n_feat)
    by_feat = user_total.reshape(n_user * n_item, n_feat, rows, rank).transpose(1, 0, 2, 3)
    scales, grad_user = tail(jnp.full((8, 128), scale), by_feat)
    grad_feat = (
        (coded.astype(jnp.float32) * scales[:, :1, :1])
        .transpose(1, 0, 2)
        .reshape(own_ranks, n_columns * width)
    )
    return (grad_user, grad_item, grad_week, grad_feat)


def solution(mesh):
    return jax.shard_map(
        local,
        mesh=mesh,
        in_specs=(
            P(("user", "item", "feat"), None, None),
            P(("user", "item", "feat"), None),
            P(("user", "item", "feat")),
            P(("user", "item"), "feat"),
            P("user", None),
            P("item", None),
            P(),
            P(("user", "item"), "feat"),
        ),
        out_specs=(
            P(("user", "item", "feat"), None),
            P(None, ("user", "item", "feat")),
            P(None, ("user", "item", "feat")),
            P(("user", "item"), "feat"),
        ),
        check_vma=False,
    )
```

```python
import jax
import jax.numpy as jnp
from jax import lax
from jax.experimental import pallas as pl
from jax.experimental.pallas import tpu as pltpu
from jax.sharding import PartitionSpec as P

BU = 256
BI = 256
BW = 64
ITEMS_STEP = 16

tensor_scale = 0.015625
side_scale = 0.03125


def tile_kernel(starts, live, tile, user, item, week, user_sum, item_sum, week_sum):
    slot = pl.program_id(0)
    step = pl.program_id(1)

    @pl.when((slot == 0) & (step == 0))
    def _():
        user_sum[...] = jnp.zeros_like(user_sum)
        item_sum[...] = jnp.zeros_like(item_sum)
        week_sum[...] = jnp.zeros_like(week_sum)

    @pl.when(live[slot] > 0)
    def _():
        user_rows = pl.ds(pl.multiple_of(starts[slot, 0], BU), BU)
        item_rows = pl.ds(
            pl.multiple_of(starts[slot, 1] + step * ITEMS_STEP, ITEMS_STEP), ITEMS_STEP
        )
        week_rows = pl.ds(pl.multiple_of(starts[slot, 2], BW), BW)
        users = user[user_rows, :]
        items = item[item_rows, :].astype(jnp.float32)
        weeks = week[week_rows, :].astype(jnp.float32)
        rank = users.shape[1]
        khatri = (
            (items[:, None, :] * weeks[None, :, :])
            .reshape(ITEMS_STEP * BW, rank)
            .astype(jnp.bfloat16)
        )
        predicted = lax.dot_general(
            users, khatri, (((1,), (1,)), ((), ())), preferred_element_type=jnp.float32
        )
        residual = (tensor_scale * (predicted - tile[0].astype(jnp.float32))).astype(
            jnp.bfloat16
        )
        user_sum[user_rows, :] += jnp.dot(residual, khatri, preferred_element_type=jnp.float32)
        crossed = lax.dot_general(
            residual, users, (((0,), (0,)), ((), ())), preferred_element_type=jnp.float32
        ).reshape(ITEMS_STEP, BW, rank)
        item_sum[item_rows, :] += jnp.sum(crossed * weeks[None, :, :], axis=1)
        week_sum[week_rows, :] += jnp.sum(crossed * items[:, None, :], axis=0)


def tile_sums(tensor_tiles, tile_coords, tile_live, user_factor, item_factor, week_factor):
    slots, _, width = tensor_tiles.shape
    rank = user_factor.shape[1]
    steps = BI // ITEMS_STEP
    starts = jnp.stack(
        [
            lax.rem(tile_coords[:, 0] * BU, user_factor.shape[0]),
            lax.rem(tile_coords[:, 1] * BI, item_factor.shape[0]),
            tile_coords[:, 2] * BW,
        ],
        axis=1,
    )

    def tile_map(s, j, starts, live):
        count = live[0]
        for k in range(1, slots):
            count += live[k]
        dead = s >= count
        return (
            jnp.where(dead, jnp.maximum(count - 1, 0), s),
            0,
            jnp.where(dead, jnp.where(count > 0, steps - 1, 0), j),
        )

    whole = lambda a: pl.BlockSpec(a.shape, lambda s, j, *_: (0, 0))
    outs = [
        jax.ShapeDtypeStruct(a.shape, jnp.float32)
        for a in (user_factor, item_factor, week_factor)
    ]
    return pl.pallas_call(
        tile_kernel,
        grid_spec=pltpu.PrefetchScalarGridSpec(
            num_scalar_prefetch=2,
            grid=(slots, steps),
            in_specs=[
                pl.BlockSpec((1, BU, ITEMS_STEP * BW), tile_map),
                whole(user_factor),
                whole(item_factor),
                whole(week_factor),
            ],
            out_specs=[whole(a) for a in outs],
        ),
        out_shape=outs,
        compiler_params=pltpu.CompilerParams(
            dimension_semantics=("arbitrary", "arbitrary"),
            vmem_limit_bytes=40 * 1024 * 1024,
        ),
        cost_estimate=pl.CostEstimate(
            flops=slots * 6 * BU * width * rank,
            bytes_accessed=slots * 2 * BU * width,
            transcendentals=0,
        ),
        name="tile_sums",
    )(starts, tile_live, tensor_tiles, user_factor, item_factor, week_factor)


def gather_rows(block, axis):
    count = lax.axis_size(axis)
    me = lax.axis_index(axis)
    rows = block.shape[0]
    whole = jnp.zeros((count * rows,) + block.shape[1:], block.dtype)
    for shift in range(count):
        piece = block
        if shift:
            piece = lax.ppermute(
                block, axis, [(k, (k + shift) % count) for k in range(count)]
            )
        whole = lax.dynamic_update_slice_in_dim(
            whole, piece, lax.rem(me - shift + count, count) * rows, 0
        )
    return whole


def peer(axes, shift):
    size = 1
    me = 0
    for axis in axes:
        size *= lax.axis_size(axis)
        me = me * lax.axis_size(axis) + lax.axis_index(axis)
    place = lax.rem(me + shift, size)
    left = place
    device = {}
    for axis in reversed(axes):
        device[axis] = lax.rem(left, lax.axis_size(axis))
        left = left // lax.axis_size(axis)
    return device, place


def tail_kernel(
    scale_in, user_in, both_in,
    scale_out, user_out, item_out, week_out,
    user_got, user_mid, user_last, both_got, both_mid, both_last,
    own_sem, scale_sems, user_sems, last_sems, both_sems, item_sems,
):
    columns = ("user", "item")
    sums = ("user", "feat")
    n_columns = scale_out.shape[0]
    n_feat = user_in.shape[0]
    n_sums = both_in.shape[0]
    n_item = both_mid.shape[0]
    me_columns = peer(columns, 0)[1]
    me_feat = lax.axis_index("feat")
    me_sums = peer(sums, 0)[1]
    me_item = lax.axis_index("item")

    barrier = pltpu.get_barrier_semaphore()
    for axes, count in ((columns, n_columns), (sums, n_sums)):
        for shift in range(1, count):
            pl.semaphore_signal(
                barrier, inc=1, device_id=peer(axes, shift)[0],
                device_id_type=pl.DeviceIdType.MESH,
            )
    pl.semaphore_wait(barrier, n_columns + n_sums - 2)

    def send(src, dst, sems, shift, device):
        copy = pltpu.make_async_remote_copy(
            src_ref=src, dst_ref=dst, send_sem=sems.at[0, shift - 1],
            recv_sem=sems.at[1, shift - 1], device_id=device,
            device_id_type=pl.DeviceIdType.MESH,
        )
        copy.start()
        return copy

    user_copies = []
    for shift in range(1, n_feat):
        device, place = peer(("feat",), shift)
        user_copies.append(
            send(user_in.at[place], user_got.at[shift - 1], user_sems, shift, device)
        )
    both_copies = []
    for shift in range(1, n_sums):
        device, place = peer(sums, shift)
        both_copies.append(
            send(both_in.at[place], both_got.at[shift - 1], both_sems, shift, device)
        )
    scale_copies = []
    for shift in range(1, n_columns):
        device, place = peer(columns, shift)
        scale_copies.append(
            send(scale_in, scale_out.at[me_columns], scale_sems, shift, device)
        )
    own = pltpu.make_async_copy(scale_in, scale_out.at[me_columns], own_sem)
    own.start()

    for copy in user_copies:
        copy.wait_recv()
    total = user_in[me_feat]
    for k in range(n_feat - 1):
        total += user_got[k]
    user_mid[...] = total
    last_copies = []
    for shift in range(1, n_columns):
        device, place = peer(columns, shift)
        last_copies.append(
            send(user_mid.at[place], user_last.at[shift - 1], last_sems, shift, device)
        )

    for copy in both_copies:
        copy.wait_recv()
    total = both_in[me_sums]
    for k in range(n_sums - 1):
        total += both_got[k]
    both_mid[...] = total
    item_copies = []
    for shift in range(1, n_item):
        device, place = peer(("item",), shift)
        item_copies.append(
            send(both_mid.at[place], both_last.at[shift - 1], item_sems, shift, device)
        )

    item_rows = item_out.shape[2]
    for copy in item_copies:
        copy.wait_recv()
    block = both_mid[me_item]
    item_out[me_item] = block[:, :item_rows]
    week = block[:, item_rows:]
    for shift in range(1, n_item):
        block = both_last[shift - 1]
        item_out[lax.rem(me_item - shift + n_item, n_item)] = block[:, :item_rows]
        week += block[:, item_rows:]
    week_out[...] = week

    for copy in last_copies:
        copy.wait_recv()
    total = user_mid[me_columns]
    for k in range(n_columns - 1):
        total += user_last[k]
    user_out[...] = total

    own.wait()
    for copy in scale_copies:
        copy.wait_recv()
    for copy in both_copies + user_copies + scale_copies + item_copies + last_copies:
        copy.wait_send()


def tail(scale_in, user_in, both_in, item_rows):
    n_feat, n_columns, rows, rank = user_in.shape
    n_sums, n_item, own, length = both_in.shape
    f32 = jnp.float32
    vmem = pl.BlockSpec(memory_space=pltpu.VMEM)
    pairs = lambda count: pltpu.SemaphoreType.DMA((2, count - 1))
    return pl.pallas_call(
        tail_kernel,
        in_specs=[vmem] * 3,
        out_specs=[vmem] * 4,
        out_shape=[
            jax.ShapeDtypeStruct((n_columns,) + scale_in.shape, f32),
            jax.ShapeDtypeStruct((rows, rank), f32),
            jax.ShapeDtypeStruct((n_item, own, item_rows), f32),
            jax.ShapeDtypeStruct((own, length - item_rows), f32),
        ],
        scratch_shapes=[
            pltpu.VMEM((n_feat - 1, n_columns, rows, rank), f32),
            pltpu.VMEM((n_columns, rows, rank), f32),
            pltpu.VMEM((n_columns - 1, rows, rank), f32),
            pltpu.VMEM((n_sums - 1, n_item, own, length), f32),
            pltpu.VMEM((n_item, own, length), f32),
            pltpu.VMEM((n_item - 1, own, length), f32),
            pltpu.SemaphoreType.DMA,
            pairs(n_columns),
            pairs(n_feat),
            pairs(n_columns),
            pairs(n_sums),
            pairs(n_item),
        ],
        compiler_params=pltpu.CompilerParams(
            collective_id=0, has_side_effects=True, vmem_limit_bytes=48 * 1024 * 1024
        ),
        cost_estimate=pl.CostEstimate(
            flops=10**9, bytes_accessed=80 * 10**6, transcendentals=0
        ),
        name="tail_exchange",
    )(scale_in, user_in, both_in)


def exchange(blocks, axes):
    return lax.all_to_all(blocks, axes, split_axis=0, concat_axis=0, tiled=True)


def local(
    tensor_tiles,
    tile_coords,
    tile_live,
    side_matrix,
    user_factor,
    item_factor,
    week_factor,
    feat_factor,
):
    user_rows, rank = user_factor.shape
    item_rows = item_factor.shape[0]
    week_rows = week_factor.shape[0]
    n_user = lax.axis_size("user")
    n_item = lax.axis_size("item")
    n_feat = lax.axis_size("feat")
    own = rank // (n_user * n_item * n_feat)
    user_base = lax.axis_index("user") * user_rows

    side_rows = side_matrix.shape[0]
    n_columns = n_user * n_item
    sent = jnp.concatenate([side_matrix, feat_factor], axis=0)
    got = lax.all_to_all(sent, ("user", "item"), split_axis=1, concat_axis=0, tiled=True)
    all_users = gather_rows(user_factor, "user")

    user_sum, item_sum, week_sum = tile_sums(
        tensor_tiles, tile_coords, tile_live, user_factor, item_factor, week_factor
    )

    got, user_sum, item_sum, week_sum = lax.optimization_barrier(
        (got, user_sum, item_sum, week_sum)
    )
    got = got.reshape(n_columns, sent.shape[0], got.shape[1])
    side_cols = got[:, :side_rows].reshape(n_columns * side_rows, got.shape[2])
    factor_cols = got[:, side_rows:].reshape(rank, got.shape[2])
    both = jnp.concatenate([item_sum, week_sum], axis=0).T
    both = both.reshape(n_user, n_item, n_feat, own, item_rows + week_rows)
    both = both.transpose(0, 2, 1, 3, 4).reshape(
        n_user * n_feat, n_item, own, item_rows + week_rows
    )

    predicted = jnp.dot(all_users, factor_cols, preferred_element_type=jnp.float32)
    side_resid = (side_scale * (predicted - side_cols.astype(jnp.float32))).astype(jnp.bfloat16)
    feat_cols = lax.dot_general(
        all_users, side_resid, (((0,), (0,)), ((), ())), preferred_element_type=jnp.float32
    )
    width = feat_cols.shape[1]
    scale = jnp.maximum(jnp.max(jnp.abs(feat_cols)), 1e-30) / 16384.0
    own_ranks = rank // n_columns
    coded = (feat_cols * (1.0 / scale)).astype(jnp.float16)
    coded = exchange(coded.reshape(n_columns, own_ranks, width), ("user", "item"))
    side_user = lax.dot_general(
        side_resid, factor_cols, (((1,), (1,)), ((), ())), preferred_element_type=jnp.float32
    )
    mine = lax.dynamic_slice_in_dim(side_user, user_base, user_rows, 0)
    user_total = lax.dynamic_update_slice_in_dim(side_user, mine + user_sum, user_base, 0)
    rows = user_total.shape[0] // (n_user * n_item * n_feat)
    by_feat = user_total.reshape(n_user * n_item, n_feat, rows, rank).transpose(1, 0, 2, 3)
    scales, grad_user, by_item, by_week = tail(
        jnp.full((8, 128), scale), by_feat, both, item_rows
    )
    grad_item = by_item.transpose(0, 2, 1).reshape(n_item * item_rows, own)
    grad_week = by_week.T
    grad_feat = (
        (coded.astype(jnp.float32) * scales[:, :1, :1])
        .transpose(1, 0, 2)
        .reshape(own_ranks, n_columns * width)
    )
    return (grad_user, grad_item, grad_week, grad_feat)


def solution(mesh):
    return jax.shard_map(
        local,
        mesh=mesh,
        in_specs=(
            P(("user", "item", "feat"), None, None),
            P(("user", "item", "feat"), None),
            P(("user", "item", "feat")),
            P(("user", "item"), "feat"),
            P("user", None),
            P("item", None),
            P(),
            P(("user", "item"), "feat"),
        ),
        out_specs=(
            P(("user", "item", "feat"), None),
            P(None, ("user", "item", "feat")),
            P(None, ("user", "item", "feat")),
            P(("user", "item"), "feat"),
        ),
        check_vma=False,
    )
```
